512 devices in a mesh: mem: 64 (over x, y, z_hi, core), tile: 8 (over z_lo).
Axes of the slice: x: 4, y: 4, z: 16 (z_hi: 2, z_lo: 8; z = z_hi * 8 + z_lo), core: 2. Of those that a mesh axis runs over, the one named last changes fastest.
Arguments:
- members: float32 [64, 6, 512, 768], P('mem', None, 'tile'), may hold values from -6 to 6
- control: float32 [6, 512, 768], P(None, 'tile', 'mem'), may hold values from -6 to 6
- air_temp: float32 [512, 768], P('tile'), may hold values from -6 to 6
- flow_codes: int32 [512, 768], P('tile'), may hold values from 0 to 7
- ocean_mask: int32 [512, 768], P('tile'), may hold values 0 or 1
Outputs:
- advanced: float32 [64, 6, 512, 768], P('mem', None, 'tile')
The draws below stay inside these ranges and needn't reach their ends.
All inputs are finite; a program needn't handle non-finite values. No bound on the sum of `ocean_mask` on one device may be relied on, other than what follows from the above.
Results may differ from the reference program's by a relative error of at most 0.00002.
Values sent between devices are 32-bit elements; how exact they have to be, the bound alone decides.
A program may use at most 64 MiB of HBM per device.

```python
import jax
import jax.numpy as jnp
from jax import lax

FIELDS = 6
COLS = 768
SUBSTEPS = 2
MEMBERS = 64
NROW = 512
N_MEM = 64


def plant(result, own_key, low, high):
    longest = result.shape.index(max(result.shape))
    spots = []
    for shift in (0, 1):
        where = [jax.random.randint(jax.random.fold_in(own_key, axis), (), 0, length) for axis, length in enumerate(result.shape)]
        where[longest] = (where[longest] + shift) % result.shape[longest]
        spots.append(tuple(where))
    return result.at[spots[0]].set(low).at[spots[1]].set(high)


def levels(own_key, dims, cuts, low, top_value):
    def one(position, blocks):
        heights = jax.random.uniform(jax.random.fold_in(jax.random.fold_in(own_key, 6), position), (blocks,), jnp.float32, low / len(cuts), top_value / len(cuts))
        return jnp.repeat(jnp.exp(heights), dims[position] // blocks).reshape((-1,) + (1,) * (len(dims) - position - 1))

    loudness = one(*cuts[0])
    for cut in cuts[1:]:
        loudness = loudness * one(*cut)
    return loudness


def bell_draw(stream_key, extent, spread, reach, shards=(), held_as=jnp.bfloat16):
    drawn = spread * jax.random.normal(stream_key, extent, jnp.float32)
    if shards:
        drawn = drawn * levels(stream_key, extent, shards, -0.22, 0.18)
    return jnp.clip(drawn, -reach, reach).astype(held_as)


def setup_inputs(seed: int = 0) -> dict:
    seeds = jax.random.split(jax.random.key(seed), 6)
    members = bell_draw(seeds[0], (MEMBERS, FIELDS, NROW, COLS), 1.0, 6.0, ((0, 64), (2, 8)), jnp.float32)
    control = bell_draw(seeds[1], (FIELDS, NROW, COLS), 1.0, 6.0, ((1, 8), (2, 64)), jnp.float32)
    air_temp = bell_draw(seeds[2], (NROW, COLS), 1.0, 6.0, ((0, 8),), jnp.float32)
    flow_codes = plant(jax.random.randint(seeds[3], (NROW, COLS), 0, 8), jax.random.fold_in(seeds[3], 1), 0, 7).astype(jnp.int32)
    ocean_mask = plant((jax.random.randint(seeds[4], (NROW, COLS), 0, 5) < 4).astype(jnp.int32), jax.random.fold_in(seeds[4], 1), 0, 1)
    return dict(members=members, control=control, air_temp=air_temp, flow_codes=flow_codes, ocean_mask=ocean_mask)


step_length = 0.5
drain_rate = 0.35
DIRECTIONS = ((0, 1), (1, 1), (1, 0), (1, -1), (0, -1), (-1, -1), (-1, 0), (-1, 1))


def thermo(fields, air_temp, wet_mask):
    ice_cover, ice_thick, snow_depth = fields[0], fields[1], fields[2]
    skin_temp, pond_depth, ocean_temp = fields[3], fields[4], fields[5]
    insulation = jax.nn.softplus(ice_thick) + 0.5 * jax.nn.softplus(snow_depth) + 0.2
    conduction = (ocean_temp - skin_temp) / insulation
    melting = jax.nn.softplus(skin_temp)
    fraction = jax.nn.sigmoid(ice_cover)
    tendency = wet_mask * step_length
    new_cover = ice_cover + tendency * (conduction - melting)
    new_thick = ice_thick + tendency * (0.5 * conduction - melting * fraction)
    new_snow = snow_depth + tendency * (0.3 * jax.nn.sigmoid(-air_temp) - 0.5 * melting)
    new_skin = skin_temp + tendency * (air_temp - skin_temp + 0.1 * conduction)
    new_ocean = ocean_temp + tendency * (0.2 * (air_temp - ocean_temp) - 0.1 * conduction * fraction)
    new_pond = pond_depth + tendency * (0.5 * melting * fraction)
    stacked = jnp.stack([new_cover, new_thick, new_snow, new_skin, new_pond, new_ocean])
    return stacked, wet_mask * drain_rate * new_pond


def inflow(out_wide, code_wide):
    row_count = out_wide.shape[0] - 2
    col_count = out_wide.shape[1]
    out_pad = jnp.pad(out_wide, ((0, 0), (1, 1)))
    code_pad = jnp.pad(code_wide, ((0, 0), (1, 1)), constant_values=-1)
    arrived = jnp.zeros((row_count, col_count), out_wide.dtype)
    for number, (row_step, col_step) in enumerate(DIRECTIONS):
        source = out_pad[1 - row_step:1 - row_step + row_count, 1 - col_step:1 - col_step + col_count]
        matches = code_pad[1 - row_step:1 - row_step + row_count, 1 - col_step:1 - col_step + col_count] == number
        arrived = arrived + jnp.where(matches, source, 0.0)
    return arrived


def advance(fields, air_temp, wet_mask, flow_codes):
    code_wide = jnp.pad(flow_codes, ((1, 1), (0, 0)), constant_values=-1)
    for substep in range(SUBSTEPS):
        stacked, outflow = thermo(fields, air_temp, wet_mask)
        arrived = inflow(jnp.pad(outflow, ((1, 1), (0, 0))), code_wide)
        new_pond = stacked[4] - outflow + wet_mask * arrived
        fields = stacked.at[4].set(new_pond)
    return fields


def reference(members, control, air_temp, flow_codes, ocean_mask):
    ensemble_mean = jnp.sum(members, axis=0) / N_MEM
    wet_mask = ocean_mask.astype(jnp.float32)

    def one_member(member):
        return advance((member - ensemble_mean) + control, air_temp, wet_mask, flow_codes)

    return lax.map(one_member, members)
```

```python
import functools

import jax
import jax.numpy as jnp
from jax import lax
from jax.experimental import pallas as pl
from jax.experimental.pallas import tpu as pltpu
from jax.sharding import PartitionSpec as P

MESH = pl.DeviceIdType.MESH
SUBSTEPS = 2
MEMBERS = 64
DIRECTIONS = ((0, 1), (1, 1), (1, 0), (1, -1), (0, -1), (-1, -1), (-1, 0), (-1, 1))
STEPS = sorted(
    ((dx, dy) for dx in range(4) for dy in range(4)),
    key=lambda s: -(min(s[0], 4 - s[0]) + min(s[1], 4 - s[1])),
)
PEERS = len(STEPS) - 1


def softplus(v):
    return jnp.maximum(v, 0.0) + jnp.log1p(jnp.exp(-jnp.abs(v)))


def sigmoid(v):
    return 1.0 / (1.0 + jnp.exp(-v))


def block(ref, half, part):
    columns = pl.ds(pl.multiple_of((part % 2) * 384, 128), 384)
    return ref.at[pl.ds(3 * half, 3), part // 2, :, columns]


def kernel(
    members, control, air_temp, flow_codes, ocean_mask, advanced,
    own, raw, shift, state, core_in, plane_in, depth_out, depth_in, strip, air, code, mask, gain, outflow,
    local_sem, core_send, core_recv, plane_send, plane_recv, depth_sem,
    gather_send, gather_recv, share_send, share_recv, edge_send, edge_recv,
):
    m, t = lax.axis_index("mem"), lax.axis_index("tile")
    x, y, z, c = m // 16, (m // 4) % 4, (m // 2) % 2, m % 2

    def device(x, y, z, c):
        return (((x * 4 + y) * 2 + z) * 2 + c, t)

    sibling = device(x, y, z, 1 - c)
    far = device(x, y, 1 - z, c)
    here = x * 4 + y
    to = [((x + dx) % 4, (y + dy) % 4) for dx, dy in STEPS]
    come = [((x + 4 - dx) % 4, (y + 4 - dy) % 4) for dx, dy in STEPS]
    goal = [a * 4 + b for a, b in to]
    origin = [a * 4 + b for a, b in come]
    above, below = (m, jnp.maximum(t - 1, 0)), (m, jnp.minimum(t + 1, 7))
    has_above, has_below = t > 0, t < 7

    loads = [
        pltpu.make_async_copy(s, d, local_sem.at[i])
        for i, (s, d) in enumerate((
            (members, own), (control, strip), (air_temp, air), (ocean_mask, mask),
            (flow_codes, code.at[pl.ds(1, 8)]), (members, raw),
        ))
    ]
    for copy in loads:
        copy.start()

    barrier = pltpu.get_barrier_semaphore()
    for target in [sibling, far] + [device(a, b, z, c) for a, b in to[:PEERS]]:
        pl.semaphore_signal(barrier, inc=1, device_id=target, device_id_type=MESH)

    @pl.when(has_above)
    def _():
        pl.semaphore_signal(barrier, inc=1, device_id=above, device_id_type=MESH)

    @pl.when(has_below)
    def _():
        pl.semaphore_signal(barrier, inc=1, device_id=below, device_id_type=MESH)

    loads[0].wait()
    loads[1].wait()
    tile_at = jnp.minimum((12 * m) // 128, 4)
    span = pl.ds(pl.multiple_of(tile_at * 128, 128), 256)
    turn = 12 * m - 128 * tile_at

    def place(r, carry):
        piece = jnp.pad(strip[r // 8, r % 8], ((0, 0), (0, 244)))
        piece = pltpu.roll(piece, turn, 1)
        own[r // 8, r % 8, :, span] = own[r // 8, r % 8, :, span] - float(MEMBERS) * piece
        return carry

    lax.fori_loop(0, 48, place, 0)
    for i in (2, 3, 4, 5):
        loads[i].wait()
    for r in range(8):
        gain[r] = 0.3 * sigmoid(-air[r])

    for edge, missing in ((0, t == 0), (9, t == 7)):
        @pl.when(missing)
        def _():
            code[edge] = jnp.full((8, 768), -1, jnp.int32)
            for s in range(SUBSTEPS):
                outflow[s, edge] = jnp.zeros((8, 768), jnp.float32)

    extra = jnp.where(has_above, 1, 0) + jnp.where(has_below, 1, 0)
    pl.semaphore_wait(barrier, PEERS + 2 + extra)

    def remote(src, dst, send, recv, target):
        return pltpu.make_async_remote_copy(
            src_ref=src, dst_ref=dst, send_sem=send, recv_sem=recv, device_id=target, device_id_type=MESH)

    def edges(buffer, slot):
        up = remote(buffer.at[1], buffer.at[9], edge_send.at[slot, 0], edge_recv.at[slot, 0], above)
        down = remote(buffer.at[8], buffer.at[0], edge_send.at[slot, 1], edge_recv.at[slot, 1], below)
        return up, down

    def start_edges(buffer, slot):
        up, down = edges(buffer, slot)
        pl.when(has_above)(up.start)
        pl.when(has_below)(down.start)

    def wait_edges(buffer, slot):
        up, down = edges(buffer, slot)

        @pl.when(has_above)
        def _():
            up.wait_send()
            down.wait_recv()

        @pl.when(has_below)
        def _():
            down.wait_send()
            up.wait_recv()

    core_copies = [
        remote(block(own, 1 - c, goal[j]), core_in.at[j], core_send.at[j], core_recv.at[j], sibling)
        for j in range(PEERS + 1)
    ]
    for copy in core_copies:
        copy.start()
    start_edges(code, 0)

    plane_copies = []
    for j in range(PEERS + 1):
        core_copies[j].wait_recv()
        core_in[j] = core_in[j] + block(own, c, goal[j])[...]
        if j < PEERS:
            copy = remote(
                core_in.at[j], plane_in.at[j], plane_send.at[j], plane_recv.at[j], device(*to[j], z, c))
            copy.start()
            plane_copies.append(copy)
    total = core_in[PEERS]
    for j in reversed(range(PEERS)):
        plane_copies[j].wait_recv()
        total = total + plane_in[j]
    depth_out[...] = total

    copy = remote(depth_out, depth_in, depth_sem.at[0], depth_sem.at[1], far)
    copy.start()
    copy.wait_recv()
    block(shift, c, here)[...] = (depth_out[...] + depth_in[...]) * (-1.0 / MEMBERS)
    copy.wait_send()

    gather_copies, share_copies = [], []
    for j in range(PEERS):
        mine = block(shift, c, here)
        copy = remote(mine, mine, gather_send.at[j], gather_recv.at[j], device(*to[j], z, c))
        copy.start()
        gather_copies.append(copy)
    for j in reversed(range(PEERS + 1)):
        part = block(shift, c, origin[j])
        if j < PEERS:
            arriving = remote(part, part, gather_send.at[j], gather_recv.at[j], sibling)
            arriving.wait_recv()
        copy = remote(part, part, share_send.at[j], share_recv.at[j], sibling)
        copy.start()
        share_copies.append(copy)
    for copy in core_copies + plane_copies + gather_copies + share_copies:
        copy.wait_send()
    for j in range(PEERS + 1):
        part = block(shift, 1 - c, origin[j])
        remote(part, part, share_send.at[j], share_recv.at[j], sibling).wait_recv()
    wait_edges(code, 0)

    column = lax.broadcasted_iota(jnp.int32, (8, 768), 1)
    for s in range(SUBSTEPS):
        def thermo(n, carry):
            r = n
            if s == 0:
                cover, thick, snow, skin, pond, ocean = [raw[f, r] + shift[f, r] for f in range(6)]
            else:
                cover, thick, snow, skin, pond, ocean = [state[f, r] for f in range(6)]
            wet = mask[r].astype(jnp.float32)
            warm = air[r]
            step = 0.5 * wet
            conduction = (ocean - skin) / (softplus(thick) + 0.5 * softplus(snow) + 0.2)
            melting = softplus(skin)
            fraction = sigmoid(cover)
            drained = melting * fraction
            state[0, r] = cover + step * (conduction - melting)
            state[1, r] = thick + step * (0.5 * conduction - drained)
            state[2, r] = snow + step * (gain[r] - 0.5 * melting)
            state[3, r] = skin + step * (warm - skin + 0.1 * conduction)
            state[5, r] = ocean + step * (0.2 * (warm - ocean) - 0.1 * conduction * fraction)
            pond = pond + step * (0.5 * drained)
            state[4, r] = pond
            outflow[s, r + 1] = 0.35 * wet * pond
            return carry

        thermo(0, 0)
        thermo(7, 0)
        start_edges(outflow.at[s], 1 + s)
        lax.fori_loop(1, 7, thermo, 0)
        if s == SUBSTEPS - 1:
            stores = [
                pltpu.make_async_copy(state.at[pl.ds(f, n)], advanced.at[pl.ds(f, n)], local_sem.at[i])
                for i, (f, n) in enumerate(((0, 4), (5, 1), (4, 1)))
            ]
            stores[0].start()
            stores[1].start()
        wait_edges(outflow.at[s], 1 + s)

        row = lax.broadcasted_iota(jnp.int32, (8, 768), 0)

        def drain(r, carry):
            flows = [outflow[s, r + d] for d in range(3)]
            codes = [code[r + d] for d in range(3)]

            def sent(number, d):
                return jnp.where(codes[d] == number, flows[d], 0.0)

            down = {dc: k for k, (dr, dc) in enumerate(DIRECTIONS) if dr == 1}
            up = {dc: k for k, (dr, dc) in enumerate(DIRECTIONS) if dr == -1}
            level = {dc: k for k, (dr, dc) in enumerate(DIRECTIONS) if dr == 0}
            sums = {}
            for dc in (-1, 0, 1):
                before = pltpu.roll(jnp.where(row == 7, sent(down[dc], 0), sent(down[dc], 1)), 1, 0)
                after = pltpu.roll(jnp.where(row == 0, sent(up[dc], 2), sent(up[dc], 1)), 7, 0)
                sums[dc] = before + after
                if dc:
                    sums[dc] = sums[dc] + sent(level[dc], 1)
            right = jnp.where(column == 0, 0.0, pltpu.roll(sums[1], 1, 1))
            left = jnp.where(column == 767, 0.0, pltpu.roll(sums[-1], 767, 1))
            arrived = sums[0] + right + left
            state[4, r] = state[4, r] - flows[1] + mask[r].astype(jnp.float32) * arrived
            return carry

        lax.fori_loop(0, 8, drain, 0)
    stores[2].start()
    for copy in stores:
        copy.wait()


def solution(mesh):
    hbm = pl.BlockSpec(memory_space=pltpu.MemorySpace.HBM)
    whole = (6, 8, 8, 768)
    f32, i32 = jnp.float32, jnp.int32
    dma = pltpu.SemaphoreType.DMA
    n = PEERS + 1

    def shards(members, control, air_temp, flow_codes, ocean_mask):
        rows = (8, 8, 768)
        result = pl.pallas_call(
            kernel,
            out_shape=jax.ShapeDtypeStruct(whole, f32),
            in_specs=[hbm] * 5,
            out_specs=hbm,
            scratch_shapes=[
                pltpu.VMEM(whole, f32), pltpu.VMEM(whole, f32), pltpu.VMEM(whole, f32), pltpu.VMEM(whole, f32),
                pltpu.VMEM((n, 3, 8, 384), f32), pltpu.VMEM((n - 1, 3, 8, 384), f32),
                pltpu.VMEM((3, 8, 384), f32), pltpu.VMEM((3, 8, 384), f32),
                pltpu.VMEM((6, 8, 8, 12), f32), pltpu.VMEM(rows, f32), pltpu.VMEM((10, 8, 768), i32),
                pltpu.VMEM(rows, i32), pltpu.VMEM(rows, f32), pltpu.VMEM((SUBSTEPS, 10, 8, 768), f32),
                dma((6,)), dma((n,)), dma((n,)), dma((n - 1,)), dma((n - 1,)), dma((2,)),
                dma((n - 1,)), dma((n - 1,)), dma((n,)), dma((n,)), dma((3, 2)), dma((3, 2)),
            ],
            compiler_params=pltpu.CompilerParams(
                collective_id=0, has_side_effects=True, vmem_limit_bytes=32 * 1024 * 1024),
            name="recentre_advance",
        )(
            members.reshape(whole), control.reshape(6, 8, 8, 12), air_temp.reshape(rows),
            flow_codes.reshape(rows), ocean_mask.reshape(rows),
        )
        return result.reshape(1, 6, 64, 768)

    tiles = P("tile", None)
    return jax.shard_map(
        shards, mesh=mesh,
        in_specs=(P("mem", None, "tile", None), P(None, "tile", "mem"), tiles, tiles, tiles),
        out_specs=P("mem", None, "tile", None), check_vma=False)
```

```python
import jax
import jax.numpy as jnp
from jax import lax
from jax.experimental import pallas as pl
from jax.experimental.pallas import tpu as pltpu
from jax.sharding import PartitionSpec as P

MESH = pl.DeviceIdType.MESH
SUBSTEPS = 2
VMEM_LIMIT = 60 * 1024 * 1024
MEMBERS = 64
DIRECTIONS = ((0, 1), (1, 1), (1, 0), (1, -1), (0, -1), (-1, -1), (-1, 0), (-1, 1))
STEPS = sorted(
    ((dx, dy) for dx in range(4) for dy in range(4)),
    key=lambda s: -(min(s[0], 4 - s[0]) + min(s[1], 4 - s[1])),
)
PEERS = len(STEPS) - 1


def softplus(v):
    return jnp.maximum(v, 0.0) + jnp.log1p(jnp.exp(-jnp.abs(v)))


def sigmoid(v):
    return 1.0 / (1.0 + jnp.exp(-v))


def block(field, part):
    columns = pl.ds(pl.multiple_of((part % 2) * 384, 128), 384)
    return field.at[part // 2, :, columns]


def of_core(i, c):
    return (3 * c, 4 - 3 * c, 5 - 3 * c)[i]


def kernel(
    members, control, air_temp, flow_codes, ocean_mask, state,
    own, raw, shift, core_in, plane_in, depth_out, depth_in, strip, air, code, mask, gain, keep, outflow,
    local_sem, core_send, core_recv, plane_send, plane_recv, depth_send, depth_recv,
    gather_send, gather_recv, share_send, share_recv, edge_send, edge_recv,
):
    m, t = lax.axis_index("mem"), lax.axis_index("tile")
    x, y, z, c = m // 16, (m // 4) % 4, (m // 2) % 2, m % 2

    def device(x, y, z, c):
        return (((x * 4 + y) * 2 + z) * 2 + c, t)

    sibling = device(x, y, z, 1 - c)
    far = device(x, y, 1 - z, c)
    here = x * 4 + y
    to = [((x + dx) % 4, (y + dy) % 4) for dx, dy in STEPS]
    come = [((x + 4 - dx) % 4, (y + 4 - dy) % 4) for dx, dy in STEPS]
    goal = [a * 4 + b for a, b in to]
    origin = [a * 4 + b for a, b in come]
    above, below = (m, jnp.maximum(t - 1, 0)), (m, jnp.minimum(t + 1, 7))
    has_above, has_below = t > 0, t < 7

    loads = [
        pltpu.make_async_copy(s, d, local_sem.at[i])
        for i, (s, d) in enumerate((
            (members, own), (control, strip), (air_temp, air), (ocean_mask, mask),
            (flow_codes, code.at[pl.ds(1, 8)]), (members, raw),
        ))
    ]
    for copy in loads:
        copy.start()

    barrier = pltpu.get_barrier_semaphore()
    for target in [sibling, far] + [device(a, b, z, c) for a, b in to[:PEERS]]:
        pl.semaphore_signal(barrier, inc=1, device_id=target, device_id_type=MESH)

    @pl.when(has_above)
    def _():
        pl.semaphore_signal(barrier, inc=1, device_id=above, device_id_type=MESH)

    @pl.when(has_below)
    def _():
        pl.semaphore_signal(barrier, inc=1, device_id=below, device_id_type=MESH)

    loads[0].wait()
    loads[1].wait()
    tile_at = jnp.minimum((12 * m) // 128, 4)
    span = pl.ds(pl.multiple_of(tile_at * 128, 128), 256)
    lane = lax.broadcasted_iota(jnp.int32, (12, 256), 1) + 128 * tile_at - 12 * m
    spread = jnp.where(lane == lax.broadcasted_iota(jnp.int32, (12, 256), 0), -float(MEMBERS), 0.0)
    for f in range(6):
        placed = lax.dot_general(
            strip[f], spread, (((0,), (0,)), ((), ())),
            precision=lax.Precision.HIGHEST, preferred_element_type=jnp.float32)
        for r in range(8):
            own[f, r, :, span] = own[f, r, :, span] + placed[8 * r:8 * r + 8]
    for i in (2, 3, 4, 5):
        loads[i].wait()
    for r in range(8):
        gain[r] = 0.3 * sigmoid(-air[r])

    for edge, missing in ((0, t == 0), (9, t == 7)):
        @pl.when(missing)
        def _():
            code[edge] = jnp.full((8, 768), -1, jnp.int32)
            for s in range(SUBSTEPS):
                outflow[s, edge] = jnp.zeros((8, 768), jnp.float32)

    extra = jnp.where(has_above, 1, 0) + jnp.where(has_below, 1, 0)
    pl.semaphore_wait(barrier, PEERS + 2 + extra)

    def remote(src, dst, send, recv, target):
        return pltpu.make_async_remote_copy(
            src_ref=src, dst_ref=dst, send_sem=send, recv_sem=recv, device_id=target, device_id_type=MESH)

    def edges(buffer, slot):
        up = remote(buffer.at[1], buffer.at[9], edge_send.at[slot, 0], edge_recv.at[slot, 0], above)
        down = remote(buffer.at[8], buffer.at[0], edge_send.at[slot, 1], edge_recv.at[slot, 1], below)
        return up, down

    def start_edges(buffer, slot):
        up, down = edges(buffer, slot)
        pl.when(has_above)(up.start)
        pl.when(has_below)(down.start)

    def wait_edges(buffer, slot):
        up, down = edges(buffer, slot)

        @pl.when(has_above)
        def _():
            up.wait_send()
            down.wait_recv()

        @pl.when(has_below)
        def _():
            down.wait_send()
            up.wait_recv()

    rounds = range(3)
    pack = plane_in.at[0]

    core_copies = [
        remote(own.at[of_core(i, 1 - c)], core_in.at[i], core_send.at[i], core_recv.at[i], sibling)
        for i in rounds
    ]
    for copy in core_copies:
        copy.start()
    start_edges(code, 0)

    for i in rounds:
        core_copies[i].wait_recv()
        for j in range(PEERS + 1):
            mine = block(core_in.at[i], goal[j])
            mine[...] = mine[...] + block(own.at[of_core(i, c)], goal[j])[...]
            if j < PEERS:
                remote(mine, plane_in.at[i, j], plane_send.at[i], plane_recv.at[i], device(*to[j], z, c)).start()

    depth_copies = [
        remote(depth_out.at[i], depth_in.at[i], depth_send.at[i], depth_recv.at[i], far) for i in rounds
    ]
    for i in rounds:
        remote(pack, pack, plane_send.at[i], plane_recv.at[i], sibling).wait_recv()
        total = block(core_in.at[i], here)[...]
        for j in range(PEERS):
            total = total + plane_in[i, j]
        depth_out[i] = total
        depth_copies[i].start()

    for i in rounds:
        depth_copies[i].wait_recv()
        mine = block(shift.at[of_core(i, c)], here)
        mine[...] = (depth_out[i] + depth_in[i]) * (-1.0 / MEMBERS)
        for j in range(PEERS):
            remote(mine, mine, gather_send.at[i], gather_recv.at[i], device(*to[j], z, c)).start()

    def share(i, c):
        field = shift.at[of_core(i, c)]
        return remote(field, field, share_send.at[i], share_recv.at[i], sibling)

    def pass_on(i):
        remote(pack, pack, gather_send.at[i], gather_recv.at[i], sibling).wait_recv()
        share(i, c).start()

    def field(f, r):
        return raw[f, r] + shift[f, r]

    def wet(r):
        return mask[r].astype(jnp.float32)

    def melt(r, carry=0):
        cover, skin = field(0, r), field(3, r)
        step = 0.5 * wet(r)
        melting = softplus(skin)
        fraction = sigmoid(cover)
        keep[0, r] = step * (melting * fraction)
        keep[1, r] = skin
        keep[2, r] = fraction
        state[0, r] = cover - step * melting
        state[2, r] = step * (gain[r] - 0.5 * melting)
        state[3, r] = skin + step * (air[r] - skin)
        return carry

    def pool(r, carry=0):
        drained = keep[0, r]
        pond = field(4, r) + 0.5 * drained
        state[4, r] = pond
        outflow[0, r + 1] = 0.35 * wet(r) * pond
        thick = field(1, r)
        state[1, r] = thick - drained
        keep[0, r] = softplus(thick) + 0.2
        return carry

    def conduct(r, carry=0):
        ocean, snow = field(5, r), field(2, r)
        step = 0.5 * wet(r)
        flux = step * ((ocean - keep[1, r]) / (keep[0, r] + 0.5 * softplus(snow)))
        state[0, r] = state[0, r] + flux
        state[1, r] = state[1, r] + 0.5 * flux
        state[2, r] = state[2, r] + snow
        state[3, r] = state[3, r] + 0.1 * flux
        state[5, r] = ocean + step * (0.2 * (air[r] - ocean)) - 0.1 * flux * keep[2, r]
        return carry

    def second(r):
        cover, thick, snow, skin, pond, ocean = [state[f, r] for f in range(6)]
        step = 0.5 * wet(r)
        warm = air[r]
        conduction = (ocean - skin) / (softplus(thick) + 0.5 * softplus(snow) + 0.2)
        melting = softplus(skin)
        fraction = sigmoid(cover)
        drained = melting * fraction
        state[0, r] = cover + step * (conduction - melting)
        state[1, r] = thick + step * (0.5 * conduction - drained)
        state[2, r] = snow + step * (gain[r] - 0.5 * melting)
        state[3, r] = skin + step * (warm - skin + 0.1 * conduction)
        state[5, r] = ocean + step * (0.2 * (warm - ocean) - 0.1 * conduction * fraction)
        pond = pond + step * (0.5 * drained)
        state[4, r] = pond
        outflow[1, r + 1] = 0.35 * wet(r) * pond

    column = lax.broadcasted_iota(jnp.int32, (8, 768), 1)
    row = lax.broadcasted_iota(jnp.int32, (8, 768), 0)
    down = {dc: k for k, (dr, dc) in enumerate(DIRECTIONS) if dr == 1}
    up = {dc: k for k, (dr, dc) in enumerate(DIRECTIONS) if dr == -1}
    level = {dc: k for k, (dr, dc) in enumerate(DIRECTIONS) if dr == 0}

    def drain(s, r):
        flows = [outflow[s, r + d] for d in range(3)]
        codes = [code[r + d] for d in range(3)]

        def sent(number, d):
            return jnp.where(codes[d] == number, flows[d], 0.0)

        sums = {}
        for dc in (-1, 0, 1):
            before = pltpu.roll(jnp.where(row == 7, sent(down[dc], 0), sent(down[dc], 1)), 1, 0)
            after = pltpu.roll(jnp.where(row == 0, sent(up[dc], 2), sent(up[dc], 1)), 7, 0)
            sums[dc] = before + after
            if dc:
                sums[dc] = sums[dc] + sent(level[dc], 1)
        right = jnp.where(column == 0, 0.0, pltpu.roll(sums[1], 1, 1))
        left = jnp.where(column == 767, 0.0, pltpu.roll(sums[-1], 767, 1))
        state[4, r] = state[4, r] - flows[1] + wet(r) * (sums[0] + right + left)

    def drain_and_second(r, carry=0):
        drain(0, r)
        second(r)
        return carry

    def drain_last(r, carry=0):
        drain(1, r)
        return carry

    pass_on(0)
    pass_on(1)
    share(0, 1 - c).wait_recv()
    lax.fori_loop(0, 8, melt, 0)
    share(1, 1 - c).wait_recv()
    pool(0)
    pool(7)
    start_edges(outflow.at[0], 1)
    pass_on(2)
    lax.fori_loop(1, 7, pool, 0)
    share(2, 1 - c).wait_recv()
    lax.fori_loop(0, 8, conduct, 0)
    wait_edges(code, 0)
    wait_edges(outflow.at[0], 1)
    drain_and_second(0)
    drain_and_second(7)
    start_edges(outflow.at[1], 2)
    lax.fori_loop(1, 7, drain_and_second, 0)
    lax.fori_loop(1, 7, drain_last, 0)
    wait_edges(outflow.at[1], 2)
    drain_last(0)
    drain_last(7)

    for i in rounds:
        core_copies[i].wait_send()
        remote(pack, pack, plane_send.at[i], plane_recv.at[i], sibling).wait_send()
        depth_copies[i].wait_send()
        remote(pack, pack, gather_send.at[i], gather_recv.at[i], sibling).wait_send()
        share(i, c).wait_send()


def solution(mesh):
    hbm = pl.BlockSpec(memory_space=pltpu.MemorySpace.HBM)
    whole = (6, 8, 8, 768)
    f32, i32 = jnp.float32, jnp.int32
    dma = pltpu.SemaphoreType.DMA

    def shards(members, control, air_temp, flow_codes, ocean_mask):
        rows = (8, 8, 768)
        result = pl.pallas_call(
            kernel,
            out_shape=jax.ShapeDtypeStruct(whole, f32),
            in_specs=[hbm] * 5,
            out_specs=pl.BlockSpec(memory_space=pltpu.VMEM),
            scratch_shapes=[
                pltpu.VMEM(whole, f32), pltpu.VMEM(whole, f32), pltpu.VMEM(whole, f32),
                pltpu.VMEM((3, *rows), f32), pltpu.VMEM((3, PEERS, 8, 384), f32),
                pltpu.VMEM((3, 8, 384), f32), pltpu.VMEM((3, 8, 384), f32),
                pltpu.VMEM((6, 12, 64), f32), pltpu.VMEM(rows, f32), pltpu.VMEM((10, 8, 768), i32),
                pltpu.VMEM(rows, i32), pltpu.VMEM(rows, f32), pltpu.VMEM((3, *rows), f32),
                pltpu.VMEM((SUBSTEPS, 10, 8, 768), f32),
                dma((6,)), *[dma((3,))] * 10, dma((3, 2)), dma((3, 2)),
            ],
            compiler_params=pltpu.CompilerParams(
                collective_id=0, has_side_effects=True, vmem_limit_bytes=VMEM_LIMIT),
            name="recentre_advance",
        )(
            members.reshape(whole), jnp.swapaxes(control, 1, 2), air_temp.reshape(rows),
            flow_codes.reshape(rows), ocean_mask.reshape(rows),
        )
        return result.reshape(1, 6, 64, 768)

    tiles = P("tile", None)
    return jax.shard_map(
        shards, mesh=mesh,
        in_specs=(P("mem", None, "tile", None), P(None, "tile", "mem"), tiles, tiles, tiles),
        out_specs=P("mem", None, "tile", None), check_vma=False)
```

```python
import jax
import jax.numpy as jnp
from jax import lax
from jax.experimental import pallas as pl
from jax.experimental.pallas import tpu as pltpu
from jax.sharding import PartitionSpec as P

MESH = pl.DeviceIdType.MESH
SUBSTEPS = 2
VMEM_LIMIT = 56 * 1024 * 1024
MEMBERS = 64
DIRECTIONS = ((0, 1), (1, 1), (1, 0), (1, -1), (0, -1), (-1, -1), (-1, 0), (-1, 1))
STEPS = sorted(
    ((dx, dy) for dx in range(4) for dy in range(4)),
    key=lambda s: -(min(s[0], 4 - s[0]) + min(s[1], 4 - s[1])),
)
PEERS = len(STEPS) - 1


def softplus(v):
    return jnp.maximum(v, 0.0) + jnp.log1p(jnp.exp(-jnp.abs(v)))


def sigmoid(v):
    return 1.0 / (1.0 + jnp.exp(-v))


def block(field, part):
    columns = pl.ds(pl.multiple_of((part % 2) * 384, 128), 384)
    return field.at[part // 2, :, columns]


def of_core(i, c):
    return (3 * c, 4 - 3 * c, 5 - 3 * c)[i]


def kernel(
    members, control, air_temp, flow_codes, ocean_mask, state,
    own, raw, shift, core_in, plane_in, depth_out, depth_in, strip, air, code, mask, gain, keep, outflow, rim, rim_in,
    local_sem, core_send, core_recv, plane_send, plane_recv, depth_send, depth_recv,
    gather_send, gather_recv, share_send, share_recv, edge_send, edge_recv,
):
    m, t = lax.axis_index("mem"), lax.axis_index("tile")
    x, y, z, c = m // 16, (m // 4) % 4, (m // 2) % 2, m % 2

    def device(x, y, z, c):
        return (((x * 4 + y) * 2 + z) * 2 + c, t)

    sibling = device(x, y, z, 1 - c)
    far = device(x, y, 1 - z, c)
    here = x * 4 + y
    to = [((x + dx) % 4, (y + dy) % 4) for dx, dy in STEPS]
    come = [((x + 4 - dx) % 4, (y + 4 - dy) % 4) for dx, dy in STEPS]
    goal = [a * 4 + b for a, b in to]
    origin = [a * 4 + b for a, b in come]
    above, below = (m, jnp.maximum(t - 1, 0)), (m, jnp.minimum(t + 1, 7))
    has_above, has_below = t > 0, t < 7

    loads = [
        pltpu.make_async_copy(s, d, local_sem.at[i])
        for i, (s, d) in enumerate((
            (members, own), (control, strip), (air_temp, air), (ocean_mask, mask),
            (flow_codes, code.at[pl.ds(1, 8)]), (members, raw),
        ))
    ]
    for copy in loads:
        copy.start()

    barrier = pltpu.get_barrier_semaphore()
    for target in [sibling, far] + [device(a, b, z, c) for a, b in to[:PEERS]]:
        pl.semaphore_signal(barrier, inc=1, device_id=target, device_id_type=MESH)

    @pl.when(has_above)
    def _():
        pl.semaphore_signal(barrier, inc=1, device_id=above, device_id_type=MESH)

    @pl.when(has_below)
    def _():
        pl.semaphore_signal(barrier, inc=1, device_id=below, device_id_type=MESH)

    loads[0].wait()
    loads[1].wait()
    tile_at = jnp.minimum((12 * m) // 128, 4)
    span = pl.ds(pl.multiple_of(tile_at * 128, 128), 256)
    lane = lax.broadcasted_iota(jnp.int32, (12, 256), 1) + 128 * tile_at - 12 * m
    spread = jnp.where(lane == lax.broadcasted_iota(jnp.int32, (12, 256), 0), -float(MEMBERS), 0.0)
    for f in range(6):
        placed = lax.dot_general(
            strip[f], spread, (((0,), (0,)), ((), ())),
            precision=lax.Precision.HIGHEST, preferred_element_type=jnp.float32)
        for r in range(8):
            own[f, r, :, span] = own[f, r, :, span] + placed[8 * r:8 * r + 8]
    for i in (2, 3, 4, 5):
        loads[i].wait()
    for r in range(8):
        gain[r] = 0.3 * sigmoid(-air[r])

    for side, edge, missing in ((0, 0, t == 0), (1, 9, t == 7)):
        @pl.when(missing)
        def _():
            code[edge] = jnp.full((8, 768), -1, jnp.int32)
            for s in range(SUBSTEPS):
                rim_in[s, side] = jnp.zeros((1, 768), jnp.float32)

    extra = jnp.where(has_above, 1, 0) + jnp.where(has_below, 1, 0)
    pl.semaphore_wait(barrier, PEERS + 2 + extra)

    def remote(src, dst, send, recv, target):
        return pltpu.make_async_remote_copy(
            src_ref=src, dst_ref=dst, send_sem=send, recv_sem=recv, device_id=target, device_id_type=MESH)

    def pair(source, goal_, slot):
        return (
            remote(source[0], goal_[1], edge_send.at[slot, 0], edge_recv.at[slot, 0], above),
            remote(source[1], goal_[0], edge_send.at[slot, 1], edge_recv.at[slot, 1], below),
        )

    def start_pair(upward, downward):
        pl.when(has_above)(upward.start)
        pl.when(has_below)(downward.start)

    def wait_pair(upward, downward):
        @pl.when(has_above)
        def _():
            upward.wait_send()
            downward.wait_recv()

        @pl.when(has_below)
        def _():
            downward.wait_send()
            upward.wait_recv()

    code_pair = pair((code.at[1], code.at[8]), (code.at[0], code.at[9]), 0)
    rim_pairs = [
        pair((rim.at[s, 0], rim.at[s, 1]), (rim_in.at[s, 0], rim_in.at[s, 1]), 1 + s) for s in range(SUBSTEPS)
    ]

    def start_rim(s):
        rim[s, 0] = outflow[s, 0, 0:1]
        rim[s, 1] = outflow[s, 7, 7:8]
        start_pair(*rim_pairs[s])

    def wait_rim(s):
        wait_pair(*rim_pairs[s])

    def wait_edges():
        wait_pair(*code_pair)

    rounds = range(3)
    pack = plane_in.at[0]

    core_copies = [
        remote(own.at[of_core(i, 1 - c)], core_in.at[i], core_send.at[i], core_recv.at[i], sibling)
        for i in rounds
    ]
    for copy in core_copies:
        copy.start()
    start_pair(*code_pair)

    for i in rounds:
        core_copies[i].wait_recv()
        for j in range(PEERS + 1):
            mine = block(core_in.at[i], goal[j])
            mine[...] = mine[...] + block(own.at[of_core(i, c)], goal[j])[...]
            if j < PEERS:
                remote(mine, plane_in.at[i, j], plane_send.at[i], plane_recv.at[i], device(*to[j], z, c)).start()

    depth_copies = [
        remote(depth_out.at[i], depth_in.at[i], depth_send.at[i], depth_recv.at[i], far) for i in rounds
    ]
    for i in rounds:
        remote(pack, pack, plane_send.at[i], plane_recv.at[i], sibling).wait_recv()
        total = block(core_in.at[i], here)[...]
        for j in range(PEERS):
            total = total + plane_in[i, j]
        depth_out[i] = total
        depth_copies[i].start()

    for i in rounds:
        depth_copies[i].wait_recv()
        mine = block(shift.at[of_core(i, c)], here)
        mine[...] = (depth_out[i] + depth_in[i]) * (-1.0 / MEMBERS)
        for j in range(PEERS):
            remote(mine, mine, gather_send.at[i], gather_recv.at[i], device(*to[j], z, c)).start()

    def share(i, c):
        field = shift.at[of_core(i, c)]
        return remote(field, field, share_send.at[i], share_recv.at[i], sibling)

    def pass_on(i):
        remote(pack, pack, gather_send.at[i], gather_recv.at[i], sibling).wait_recv()
        share(i, c).start()

    def field(f, r):
        return raw[f, r] + shift[f, r]

    def wet(r):
        return mask[r].astype(jnp.float32)

    def melt(r, carry=0):
        cover, skin = field(0, r), field(3, r)
        step = 0.5 * wet(r)
        melting = softplus(skin)
        fraction = sigmoid(cover)
        keep[0, r] = step * (melting * fraction)
        keep[1, r] = skin
        keep[2, r] = fraction
        state[0, r] = cover - step * melting
        state[2, r] = step * (gain[r] - 0.5 * melting)
        state[3, r] = skin + step * (air[r] - skin)
        return carry

    def pool(r, carry=0):
        drained = keep[0, r]
        pond = field(4, r) + 0.5 * drained
        state[4, r] = pond
        outflow[0, r] = 0.35 * wet(r) * pond
        thick = field(1, r)
        state[1, r] = thick - drained
        keep[0, r] = softplus(thick) + 0.2
        return carry

    def finish(r, carry=0):
        ocean, snow, skin, fraction = field(5, r), field(2, r), keep[1, r], keep[2, r]
        step = 0.5 * wet(r)
        warm = air[r]
        flux = step * ((ocean - skin) / (keep[0, r] + 0.5 * softplus(snow)))
        cover = state[0, r] + flux
        thick = state[1, r] + 0.5 * flux
        snow = state[2, r] + snow
        skin = state[3, r] + 0.1 * flux
        ocean = ocean + step * (0.2 * (warm - ocean)) - 0.1 * flux * fraction
        conduction = (ocean - skin) / (softplus(thick) + 0.5 * softplus(snow) + 0.2)
        melting = softplus(skin)
        fraction = sigmoid(cover)
        drained = melting * fraction
        state[0, r] = cover + step * (conduction - melting)
        state[1, r] = thick + step * (0.5 * conduction - drained)
        state[2, r] = snow + step * (gain[r] - 0.5 * melting)
        state[3, r] = skin + step * (warm - skin + 0.1 * conduction)
        state[5, r] = ocean + step * (0.2 * (warm - ocean) - 0.1 * conduction * fraction)
        pond = state[4, r] + step * (0.5 * drained)
        state[4, r] = pond
        outflow[1, r] = 0.35 * wet(r) * pond
        return carry

    column = lax.broadcasted_iota(jnp.int32, (8, 768), 1)
    row = lax.broadcasted_iota(jnp.int32, (8, 768), 0)
    down = {dc: k for k, (dr, dc) in enumerate(DIRECTIONS) if dr == 1}
    up = {dc: k for k, (dr, dc) in enumerate(DIRECTIONS) if dr == -1}
    level = {dc: k for k, (dr, dc) in enumerate(DIRECTIONS) if dr == 0}

    def drain(s, r):
        def flow(d):
            if isinstance(r, int) and r + d in (-1, 8):
                return jnp.broadcast_to(rim_in[s, 0 if d < 0 else 1], (8, 768))
            return outflow[s, r + d]

        flows = [flow(d) for d in (-1, 0, 1)]
        codes = [code[r + d] for d in range(3)]

        def sent(number, d):
            return jnp.where(codes[d] == number, flows[d], 0.0)

        sums = {}
        for dc in (-1, 0, 1):
            before = pltpu.roll(jnp.where(row == 7, sent(down[dc], 0), sent(down[dc], 1)), 1, 0)
            after = pltpu.roll(jnp.where(row == 0, sent(up[dc], 2), sent(up[dc], 1)), 7, 0)
            sums[dc] = before + after
            if dc:
                sums[dc] = sums[dc] + sent(level[dc], 1)
        right = jnp.where(column == 0, 0.0, pltpu.roll(sums[1], 1, 1))
        left = jnp.where(column == 767, 0.0, pltpu.roll(sums[-1], 767, 1))
        state[4, r] = state[4, r] - flows[1] + wet(r) * (sums[0] + right + left)

    def drain_first(r, carry=0):
        drain(0, r)
        return carry

    def drain_last(r, carry=0):
        drain(1, r)
        return carry

    pass_on(0)
    pass_on(1)
    share(0, 1 - c).wait_recv()
    lax.fori_loop(0, 8, melt, 0)
    share(1, 1 - c).wait_recv()
    pool(0)
    pool(7)
    start_rim(0)
    pass_on(2)
    lax.fori_loop(1, 7, pool, 0)
    lax.fori_loop(1, 7, drain_first, 0)
    wait_edges()
    share(2, 1 - c).wait_recv()
    wait_rim(0)
    for r in (0, 7):
        drain(0, r)
        finish(r)
    start_rim(1)
    lax.fori_loop(1, 7, finish, 0)
    lax.fori_loop(1, 7, drain_last, 0)
    wait_rim(1)
    drain(1, 0)
    drain(1, 7)

    for i in rounds:
        core_copies[i].wait_send()
        remote(pack, pack, plane_send.at[i], plane_recv.at[i], sibling).wait_send()
        depth_copies[i].wait_send()
        remote(pack, pack, gather_send.at[i], gather_recv.at[i], sibling).wait_send()
        share(i, c).wait_send()


def solution(mesh):
    hbm = pl.BlockSpec(memory_space=pltpu.MemorySpace.HBM)
    whole = (6, 8, 8, 768)
    f32, i32 = jnp.float32, jnp.int32
    dma = pltpu.SemaphoreType.DMA

    def shards(members, control, air_temp, flow_codes, ocean_mask):
        rows = (8, 8, 768)
        result = pl.pallas_call(
            kernel,
            out_shape=pltpu.VMEM(whole, f32),
            in_specs=[hbm] * 5,
            out_specs=pl.BlockSpec(memory_space=pltpu.VMEM),
            scratch_shapes=[
                pltpu.VMEM(whole, f32), pltpu.VMEM(whole, f32), pltpu.VMEM(whole, f32),
                pltpu.VMEM((3, *rows), f32), pltpu.VMEM((3, PEERS, 8, 384), f32),
                pltpu.VMEM((3, 8, 384), f32), pltpu.VMEM((3, 8, 384), f32),
                pltpu.VMEM((6, 12, 64), f32), pltpu.VMEM(rows, f32), pltpu.VMEM((10, 8, 768), i32),
                pltpu.VMEM(rows, i32), pltpu.VMEM(rows, f32), pltpu.VMEM((3, *rows), f32),
                pltpu.VMEM((SUBSTEPS, 8, 8, 768), f32),
                pltpu.VMEM((SUBSTEPS, 2, 1, 768), f32), pltpu.VMEM((SUBSTEPS, 2, 1, 768), f32),
                dma((6,)), *[dma((3,))] * 10, dma((3, 2)), dma((3, 2)),
            ],
            compiler_params=pltpu.CompilerParams(
                collective_id=0, has_side_effects=True, vmem_limit_bytes=VMEM_LIMIT),
            name="recentre_advance",
        )(
            members.reshape(whole), jnp.swapaxes(control, 1, 2), air_temp.reshape(rows),
            flow_codes.reshape(rows), ocean_mask.reshape(rows),
        )
        return result.reshape(1, 6, 64, 768)

    tiles = P("tile", None)
    return jax.shard_map(
        shards, mesh=mesh,
        in_specs=(P("mem", None, "tile", None), P(None, "tile", "mem"), tiles, tiles, tiles),
        out_specs=P("mem", None, "tile", None), check_vma=False)
```

```python
import jax
import jax.numpy as jnp
from jax import lax
from jax.experimental import pallas as pl
from jax.experimental.pallas import tpu as pltpu
from jax.sharding import PartitionSpec as P

MESH = pl.DeviceIdType.MESH
SUBSTEPS = 2
VMEM_LIMIT = 56 * 1024 * 1024
MEMBERS = 64
DIRECTIONS = ((0, 1), (1, 1), (1, 0), (1, -1), (0, -1), (-1, -1), (-1, 0), (-1, 1))
STEPS = sorted(
    ((dx, dy) for dx in range(4) for dy in range(4)),
    key=lambda s: -(min(s[0], 4 - s[0]) + min(s[1], 4 - s[1])),
)
PEERS = len(STEPS) - 1


def softplus(v):
    return jnp.maximum(v, 0.0) + jnp.log1p(jnp.exp(-jnp.abs(v)))


def sigmoid(v):
    return 1.0 / (1.0 + jnp.exp(-v))


def block(field, part):
    columns = pl.ds(pl.multiple_of((part % 2) * 384, 128), 384)
    return field.at[part // 2, :, columns]


def of_core(i, c):
    return (3 * c, 4 - 3 * c, 5 - 3 * c)[i]


def kernel(
    members, control, air_temp, flow_codes, ocean_mask, state,
    own, raw, shift, core_in, plane_in, depth_out, depth_in, strip, air, code, mask, gain, keep, outflow, rim, rim_in,
    local_sem, core_send, core_recv, plane_send, plane_recv, depth_send, depth_recv,
    gather_send, gather_recv, share_send, share_recv, edge_send, edge_recv, last_recv, outer_send, outer_recv,
):
    m, t = lax.axis_index("mem"), lax.axis_index("tile")
    x, y, z, c = m // 16, (m // 4) % 4, (m // 2) % 2, m % 2

    def device(x, y, z, c):
        return (((x * 4 + y) * 2 + z) * 2 + c, t)

    sibling = device(x, y, z, 1 - c)
    far = device(x, y, 1 - z, c)
    here = x * 4 + y
    to = [((x + dx) % 4, (y + dy) % 4) for dx, dy in STEPS]
    come = [((x + 4 - dx) % 4, (y + 4 - dy) % 4) for dx, dy in STEPS]
    goal = [a * 4 + b for a, b in to]
    origin = [a * 4 + b for a, b in come]
    above, below = (m, jnp.maximum(t - 1, 0)), (m, jnp.minimum(t + 1, 7))
    has_above, has_below = t > 0, t < 7

    def greet(sem, target):
        pl.semaphore_signal(sem, inc=1, device_id=target, device_id_type=MESH)

    everyone = [far, *(device(a, b, z, c) for a, b in to[:PEERS]), sibling]
    barrier = pltpu.get_barrier_semaphore()
    for target in everyone:
        greet(barrier, target)

    @pl.when(has_above)
    def _():
        greet(barrier, above)

    @pl.when(has_below)
    def _():
        greet(barrier, below)

    loads = [
        pltpu.make_async_copy(s, d, local_sem.at[i])
        for i, (s, d) in enumerate((
            (members, own), (control, strip), (air_temp, air), (ocean_mask, mask),
            (flow_codes, code.at[pl.ds(1, 8)]), (members, raw),
        ))
    ]
    for copy in loads[:2]:
        copy.start()

    loads[0].wait()
    loads[1].wait()
    tile_at = jnp.minimum((12 * m) // 128, 4)
    span = pl.ds(pl.multiple_of(tile_at * 128, 128), 256)
    lane = lax.broadcasted_iota(jnp.int32, (12, 256), 1) + 128 * tile_at - 12 * m
    spread = jnp.where(lane == lax.broadcasted_iota(jnp.int32, (12, 256), 0), -float(MEMBERS), 0.0)
    for f in range(6):
        placed = lax.dot_general(
            strip[f], spread, (((0,), (0,)), ((), ())),
            precision=lax.Precision.HIGHEST, preferred_element_type=jnp.float32)
        for r in range(8):
            own[f, r, :, span] = own[f, r, :, span] + placed[8 * r:8 * r + 8]
    for copy in loads[2:]:
        copy.start()
    extra = jnp.where(has_above, 1, 0) + jnp.where(has_below, 1, 0)
    pl.semaphore_wait(barrier, PEERS + 2 + extra)

    def remote(src, dst, send, recv, target):
        return pltpu.make_async_remote_copy(
            src_ref=src, dst_ref=dst, send_sem=send, recv_sem=recv, device_id=target, device_id_type=MESH)

    def pair(source, goal_, slot):
        return (
            remote(source[0], goal_[1], edge_send.at[slot, 0], edge_recv.at[slot, 0], above),
            remote(source[1], goal_[0], edge_send.at[slot, 1], edge_recv.at[slot, 1], below),
        )

    def start_pair(upward, downward):
        pl.when(has_above)(upward.start)
        pl.when(has_below)(downward.start)

    def wait_pair(upward, downward):
        @pl.when(has_above)
        def _():
            upward.wait_send()
            downward.wait_recv()

        @pl.when(has_below)
        def _():
            downward.wait_send()
            upward.wait_recv()

    code_pair = pair((code.at[1], code.at[8]), (code.at[0], code.at[9]), 0)
    rim_pairs = [
        pair((rim.at[s, 0], rim.at[s, 1]), (rim_in.at[s, 0], rim_in.at[s, 1]), 1 + s) for s in range(SUBSTEPS)
    ]

    def start_rim(s):
        rim[s, 0] = outflow[s, 0, 0:1]
        rim[s, 1] = outflow[s, 7, 7:8]
        start_pair(*rim_pairs[s])

    def wait_rim(s):
        wait_pair(*rim_pairs[s])

    def wait_edges():
        wait_pair(*code_pair)

    rounds = range(3)
    pack = plane_in.at[0]

    core_copies = [
        remote(own.at[of_core(i, 1 - c)], core_in.at[i], core_send.at[i], core_recv.at[i], sibling)
        for i in rounds
    ]
    for copy in core_copies:
        copy.start()

    for i in rounds:
        core_copies[i].wait_recv()
        for j in range(PEERS + 1):
            mine = block(core_in.at[i], goal[j])
            mine[...] = mine[...] + block(own.at[of_core(i, c)], goal[j])[...]
            if j < PEERS:
                remote(mine, plane_in.at[i, j], plane_send.at[i], plane_recv.at[i], device(*to[j], z, c)).start()


    for i in (2, 3, 4, 5):
        loads[i].wait()
    for r in range(8):
        gain[r] = 0.3 * sigmoid(-air[r])

    for side, edge, missing in ((0, 0, t == 0), (1, 9, t == 7)):
        @pl.when(missing)
        def _():
            code[edge] = jnp.full((8, 768), -1, jnp.int32)
            for s in range(SUBSTEPS):
                rim_in[s, side] = jnp.zeros((1, 768), jnp.float32)

    start_pair(*code_pair)

    depth_copies = [
        remote(depth_out.at[i], depth_in.at[i], depth_send.at[i], depth_recv.at[i], far) for i in rounds
    ]
    for i in rounds:
        remote(pack, pack, plane_send.at[i], plane_recv.at[i], sibling).wait_recv()
        total = block(core_in.at[i], here)[...]
        for j in range(PEERS):
            total = total + plane_in[i, j]
        depth_out[i] = total
        depth_copies[i].start()

    for i in rounds:
        depth_copies[i].wait_recv()
        mine = block(shift.at[of_core(i, c)], here)
        mine[...] = (depth_out[i] + depth_in[i]) * (-1.0 / MEMBERS)
        for j in range(PEERS):
            landed = gather_recv.at[i] if i < 2 else last_recv.at[j]
            remote(mine, mine, gather_send.at[i], landed, device(*to[j], z, c)).start()
        if i == 2:
            remote(mine, mine, share_send.at[i], share_recv.at[i], sibling).start()

    def share(i, c):
        part = shift.at[of_core(i, c)]
        if i == 1:
            part = shift.at[of_core(i, c), pl.ds(1, 6)]
        return remote(part, part, share_send.at[i], share_recv.at[i], sibling)

    def share_outer(k, c):
        part = shift.at[of_core(1, c), 7 * k]
        return remote(part, part, outer_send.at[k], outer_recv.at[k], sibling)

    def pass_on(i):
        remote(pack, pack, gather_send.at[i], gather_recv.at[i], sibling).wait_recv()
        if i == 1:
            share_outer(0, c).start()
            share_outer(1, c).start()
        share(i, c).start()

    def pass_on_last():
        for j in range(PEERS):
            part = block(shift.at[of_core(2, c)], origin[j])
            remote(part, part, share_send.at[2], last_recv.at[j], sibling).wait_recv()
            remote(part, part, share_send.at[2], share_recv.at[2], sibling).start()

    def field(f, r):
        return raw[f, r] + shift[f, r]

    def wet(r):
        return mask[r].astype(jnp.float32)

    def melt(r, carry=0):
        cover, skin = field(0, r), field(3, r)
        step = 0.5 * wet(r)
        melting = softplus(skin)
        fraction = sigmoid(cover)
        keep[0, r] = step * (melting * fraction)
        keep[1, r] = skin
        keep[2, r] = fraction
        state[0, r] = cover - step * melting
        state[2, r] = step * (gain[r] - 0.5 * melting)
        state[3, r] = skin + step * (air[r] - skin)
        return carry

    def pool(r, carry=0):
        drained = keep[0, r]
        pond = field(4, r) + 0.5 * drained
        state[4, r] = pond
        outflow[0, r] = 0.35 * wet(r) * pond
        thick = field(1, r)
        state[1, r] = thick - drained
        keep[0, r] = softplus(thick) + 0.2
        return carry

    def finish(r, carry=0):
        ocean, snow, skin, fraction = field(5, r), field(2, r), keep[1, r], keep[2, r]
        step = 0.5 * wet(r)
        warm = air[r]
        flux = step * ((ocean - skin) / (keep[0, r] + 0.5 * softplus(snow)))
        cover = state[0, r] + flux
        thick = state[1, r] + 0.5 * flux
        snow = state[2, r] + snow
        skin = state[3, r] + 0.1 * flux
        ocean = ocean + step * (0.2 * (warm - ocean)) - 0.1 * flux * fraction
        conduction = (ocean - skin) / (softplus(thick) + 0.5 * softplus(snow) + 0.2)
        melting = softplus(skin)
        fraction = sigmoid(cover)
        drained = melting * fraction
        state[0, r] = cover + step * (conduction - melting)
        state[1, r] = thick + step * (0.5 * conduction - drained)
        state[2, r] = snow + step * (gain[r] - 0.5 * melting)
        state[3, r] = skin + step * (warm - skin + 0.1 * conduction)
        state[5, r] = ocean + step * (0.2 * (warm - ocean) - 0.1 * conduction * fraction)
        keep[0, r] = step * (0.5 * drained)
        return carry

    def settle(r):
        pond = state[4, r] + keep[0, r]
        state[4, r] = pond
        outflow[1, r] = 0.35 * wet(r) * pond

    def finish_and_settle(r, carry=0):
        finish(r)
        settle(r)
        return carry

    column = lax.broadcasted_iota(jnp.int32, (8, 768), 1)
    row = lax.broadcasted_iota(jnp.int32, (8, 768), 0)
    down = {dc: k for k, (dr, dc) in enumerate(DIRECTIONS) if dr == 1}
    up = {dc: k for k, (dr, dc) in enumerate(DIRECTIONS) if dr == -1}
    level = {dc: k for k, (dr, dc) in enumerate(DIRECTIONS) if dr == 0}

    def drain(s, r):
        def flow(d):
            if isinstance(r, int) and r + d in (-1, 8):
                return jnp.broadcast_to(rim_in[s, 0 if d < 0 else 1], (8, 768))
            return outflow[s, r + d]

        flows = [flow(d) for d in (-1, 0, 1)]
        codes = [code[r + d] for d in range(3)]

        def sent(number, d):
            return jnp.where(codes[d] == number, flows[d], 0.0)

        sums = {}
        for dc in (-1, 0, 1):
            before = pltpu.roll(jnp.where(row == 7, sent(down[dc], 0), sent(down[dc], 1)), 1, 0)
            after = pltpu.roll(jnp.where(row == 0, sent(up[dc], 2), sent(up[dc], 1)), 7, 0)
            sums[dc] = before + after
            if dc:
                sums[dc] = sums[dc] + sent(level[dc], 1)
        right = jnp.where(column == 0, 0.0, pltpu.roll(sums[1], 1, 1))
        left = jnp.where(column == 767, 0.0, pltpu.roll(sums[-1], 767, 1))
        state[4, r] = state[4, r] - flows[1] + wet(r) * (sums[0] + right + left)

    def drain_first(r, carry=0):
        drain(0, r)
        return carry

    def drain_last(r, carry=0):
        drain(1, r)
        return carry

    pass_on(0)
    share(0, 1 - c).wait_recv()
    melt(0)
    melt(7)
    pass_on(1)
    lax.fori_loop(1, 7, melt, 0)
    for k in (0, 1):
        share_outer(k, 1 - c).wait_recv()
        pool(7 * k)
    start_rim(0)
    share(1, 1 - c).wait_recv()
    pass_on_last()
    lax.fori_loop(1, 7, pool, 0)
    wait_edges()
    lax.fori_loop(1, 7, drain_first, 0)
    share(2, 1 - c).wait_recv()
    finish(0)
    finish(7)
    wait_rim(0)
    for r in (0, 7):
        drain(0, r)
        settle(r)
    start_rim(1)
    lax.fori_loop(1, 7, finish_and_settle, 0)
    lax.fori_loop(1, 7, drain_last, 0)
    wait_rim(1)
    drain(1, 0)
    drain(1, 7)

    for i in rounds:
        core_copies[i].wait_send()
        remote(pack, pack, plane_send.at[i], plane_recv.at[i], sibling).wait_send()
        depth_copies[i].wait_send()
        remote(pack, pack, gather_send.at[i], gather_recv.at[i], sibling).wait_send()
        share(i, c).wait_send()
    share_outer(0, c).wait_send()
    share_outer(1, c).wait_send()


def solution(mesh):
    hbm = pl.BlockSpec(memory_space=pltpu.MemorySpace.HBM)
    whole = (6, 8, 8, 768)
    f32, i32 = jnp.float32, jnp.int32
    dma = pltpu.SemaphoreType.DMA

    def shards(members, control, air_temp, flow_codes, ocean_mask):
        rows = (8, 8, 768)
        result = pl.pallas_call(
            kernel,
            out_shape=pltpu.VMEM(whole, f32),
            in_specs=[hbm] * 5,
            out_specs=pl.BlockSpec(memory_space=pltpu.VMEM),
            scratch_shapes=[
                pltpu.VMEM(whole, f32), pltpu.VMEM(whole, f32), pltpu.VMEM(whole, f32),
                pltpu.VMEM((3, *rows), f32), pltpu.VMEM((3, PEERS, 8, 384), f32),
                pltpu.VMEM((3, 8, 384), f32), pltpu.VMEM((3, 8, 384), f32),
                pltpu.VMEM((6, 12, 64), f32), pltpu.VMEM(rows, f32), pltpu.VMEM((10, 8, 768), i32),
                pltpu.VMEM(rows, i32), pltpu.VMEM(rows, f32), pltpu.VMEM((3, *rows), f32),
                pltpu.VMEM((SUBSTEPS, 8, 8, 768), f32),
                pltpu.VMEM((SUBSTEPS, 2, 1, 768), f32), pltpu.VMEM((SUBSTEPS, 2, 1, 768), f32),
                dma((6,)), *[dma((3,))] * 10, dma((3, 2)), dma((3, 2)),
                dma((PEERS,)),
                dma((2,)), dma((2,)),
            ],
            compiler_params=pltpu.CompilerParams(
                collective_id=0, has_side_effects=True, vmem_limit_bytes=VMEM_LIMIT),
            name="recentre_advance",
        )(
            members.reshape(whole), jnp.swapaxes(control, 1, 2), air_temp.reshape(rows),
            flow_codes.reshape(rows), ocean_mask.reshape(rows),
        )
        return result.reshape(1, 6, 64, 768)

    tiles = P("tile", None)
    return jax.shard_map(
        shards, mesh=mesh,
        in_specs=(P("mem", None, "tile", None), P(None, "tile", "mem"), tiles, tiles, tiles),
        out_specs=P("mem", None, "tile", None), check_vma=False)
```

```python
import jax
import jax.numpy as jnp
from jax import lax
from jax.experimental import pallas as pl
from jax.experimental.pallas import tpu as pltpu
from jax.sharding import PartitionSpec as P

MESH = pl.DeviceIdType.MESH
SUBSTEPS = 2
VMEM_LIMIT = 56 * 1024 * 1024
MEMBERS = 64
DIRECTIONS = ((0, 1), (1, 1), (1, 0), (1, -1), (0, -1), (-1, -1), (-1, 0), (-1, 1))
STEPS = sorted(
    ((dx, dy) for dx in range(4) for dy in range(4)),
    key=lambda s: -(min(s[0], 4 - s[0]) + min(s[1], 4 - s[1])),
)
PEERS = len(STEPS) - 1


def softplus(v):
    return jnp.maximum(v, 0.0) + jnp.log(1.0 + jnp.exp(-jnp.abs(v)))


def sigmoid(v):
    return 1.0 / (1.0 + jnp.exp(-v))


def block(field, part):
    columns = pl.ds(pl.multiple_of((part % 2) * 384, 128), 384)
    return field.at[part // 2, :, columns]


def of_core(i, c):
    return (3 * c, 4 - 3 * c, 5 - 3 * c)[i]


def kernel(
    members, control, air_temp, flow_codes, ocean_mask, state,
    own, raw, shift, core_in, plane_in, depth_out, depth_in, strip, air, code, mask, gain, keep, outflow, rim, rim_in,
    local_sem, core_send, core_recv, plane_send, plane_recv, depth_send, depth_recv,
    gather_send, gather_recv, share_send, share_recv, edge_send, edge_recv, last_recv, outer_send, outer_recv,
):
    m, t = lax.axis_index("mem"), lax.axis_index("tile")
    x, y, z, c = m // 16, (m // 4) % 4, (m // 2) % 2, m % 2

    def device(x, y, z, c):
        return (((x * 4 + y) * 2 + z) * 2 + c, t)

    sibling = device(x, y, z, 1 - c)
    far = device(x, y, 1 - z, c)
    here = x * 4 + y
    to = [((x + dx) % 4, (y + dy) % 4) for dx, dy in STEPS]
    come = [((x + 4 - dx) % 4, (y + 4 - dy) % 4) for dx, dy in STEPS]
    goal = [a * 4 + b for a, b in to]
    origin = [a * 4 + b for a, b in come]
    above, below = (m, jnp.maximum(t - 1, 0)), (m, jnp.minimum(t + 1, 7))
    has_above, has_below = t > 0, t < 7

    def greet(sem, target):
        pl.semaphore_signal(sem, inc=1, device_id=target, device_id_type=MESH)

    everyone = [far, *(device(a, b, z, c) for a, b in to[:PEERS]), sibling]
    barrier = pltpu.get_barrier_semaphore()
    for target in everyone:
        greet(barrier, target)

    @pl.when(has_above)
    def _():
        greet(barrier, above)

    @pl.when(has_below)
    def _():
        greet(barrier, below)

    loads = [
        pltpu.make_async_copy(s, d, local_sem.at[i])
        for i, (s, d) in enumerate((
            (members, own), (control, strip), (air_temp, air), (ocean_mask, mask),
            (flow_codes, code.at[pl.ds(1, 8)]), (members, raw),
        ))
    ]
    for copy in loads[:2]:
        copy.start()

    loads[0].wait()
    loads[1].wait()
    tile_at = jnp.minimum((12 * m) // 128, 4)
    span = pl.ds(pl.multiple_of(tile_at * 128, 128), 256)
    lane = lax.broadcasted_iota(jnp.int32, (12, 256), 1) + 128 * tile_at - 12 * m
    spread = jnp.where(lane == lax.broadcasted_iota(jnp.int32, (12, 256), 0), -float(MEMBERS), 0.0)
    for f in range(6):
        placed = lax.dot_general(
            strip[f], spread, (((0,), (0,)), ((), ())),
            precision=lax.Precision.HIGHEST, preferred_element_type=jnp.float32)
        for r in range(8):
            own[f, r, :, span] = own[f, r, :, span] + placed[8 * r:8 * r + 8]
    for copy in loads[2:]:
        copy.start()
    extra = jnp.where(has_above, 1, 0) + jnp.where(has_below, 1, 0)
    pl.semaphore_wait(barrier, PEERS + 2 + extra)

    def remote(src, dst, send, recv, target):
        return pltpu.make_async_remote_copy(
            src_ref=src, dst_ref=dst, send_sem=send, recv_sem=recv, device_id=target, device_id_type=MESH)

    def pair(source, goal_, slot):
        return (
            remote(source[0], goal_[1], edge_send.at[slot, 0], edge_recv.at[slot, 0], above),
            remote(source[1], goal_[0], edge_send.at[slot, 1], edge_recv.at[slot, 1], below),
        )

    def start_pair(upward, downward):
        pl.when(has_above)(upward.start)
        pl.when(has_below)(downward.start)

    def wait_pair(upward, downward):
        @pl.when(has_above)
        def _():
            upward.wait_send()
            downward.wait_recv()

        @pl.when(has_below)
        def _():
            downward.wait_send()
            upward.wait_recv()

    code_pair = pair((code.at[1], code.at[8]), (code.at[0], code.at[9]), 0)
    rim_pairs = [
        pair((rim.at[s, 0], rim.at[s, 1]), (rim_in.at[s, 0], rim_in.at[s, 1]), 1 + s) for s in range(SUBSTEPS)
    ]

    def start_rim(s):
        rim[s, 0] = outflow[s, 0, 0:1]
        rim[s, 1] = outflow[s, 7, 7:8]
        start_pair(*rim_pairs[s])

    def wait_rim(s):
        wait_pair(*rim_pairs[s])

    def wait_edges():
        wait_pair(*code_pair)

    rounds = range(3)
    pack = plane_in.at[0]

    core_copies = [
        remote(own.at[of_core(i, 1 - c)], core_in.at[i], core_send.at[i], core_recv.at[i], sibling)
        for i in rounds
    ]
    for copy in core_copies:
        copy.start()

    for i in rounds:
        core_copies[i].wait_recv()
        for j in range(PEERS + 1):
            mine = block(core_in.at[i], goal[j])
            mine[...] = mine[...] + block(own.at[of_core(i, c)], goal[j])[...]
            if j < PEERS:
                remote(mine, plane_in.at[i, j], plane_send.at[i], plane_recv.at[i], device(*to[j], z, c)).start()


    for i in (2, 3, 4, 5):
        loads[i].wait()
    for r in range(8):
        gain[r] = 0.3 * sigmoid(-air[r])

    for side, edge, missing in ((0, 0, t == 0), (1, 9, t == 7)):
        @pl.when(missing)
        def _():
            code[edge] = jnp.full((8, 768), -1, jnp.int32)
            for s in range(SUBSTEPS):
                rim_in[s, side] = jnp.zeros((1, 768), jnp.float32)

    start_pair(*code_pair)

    depth_copies = [
        remote(depth_out.at[i], depth_in.at[i], depth_send.at[i], depth_recv.at[i], far) for i in rounds
    ]
    for i in rounds:
        remote(pack, pack, plane_send.at[i], plane_recv.at[i], sibling).wait_recv()
        total = block(core_in.at[i], here)[...]
        for j in range(PEERS):
            total = total + plane_in[i, j]
        depth_out[i] = total
        depth_copies[i].start()

    for i in rounds:
        depth_copies[i].wait_recv()
        mine = block(shift.at[of_core(i, c)], here)
        mine[...] = (depth_out[i] + depth_in[i]) * (-1.0 / MEMBERS)
        for j in range(PEERS):
            landed = gather_recv.at[i] if i < 2 else last_recv.at[j]
            remote(mine, mine, gather_send.at[i], landed, device(*to[j], z, c)).start()
        if i == 2:
            remote(mine, mine, share_send.at[i], share_recv.at[i], sibling).start()

    def share(i, c):
        part = shift.at[of_core(i, c)]
        if i == 1:
            part = shift.at[of_core(i, c), pl.ds(1, 6)]
        return remote(part, part, share_send.at[i], share_recv.at[i], sibling)

    def share_outer(k, c):
        part = shift.at[of_core(1, c), 7 * k]
        return remote(part, part, outer_send.at[k], outer_recv.at[k], sibling)

    def pass_on(i):
        remote(pack, pack, gather_send.at[i], gather_recv.at[i], sibling).wait_recv()
        if i == 1:
            share_outer(0, c).start()
            share_outer(1, c).start()
        share(i, c).start()

    def pass_on_last():
        for j in range(PEERS):
            part = block(shift.at[of_core(2, c)], origin[j])
            remote(part, part, share_send.at[2], last_recv.at[j], sibling).wait_recv()
            remote(part, part, share_send.at[2], share_recv.at[2], sibling).start()

    def field(f, r):
        return raw[f, r] + shift[f, r]

    def wet(r):
        return mask[r].astype(jnp.float32)

    def melt(r, carry=0):
        cover, skin = field(0, r), field(3, r)
        step = 0.5 * wet(r)
        melting = softplus(skin)
        fraction = sigmoid(cover)
        keep[0, r] = step * (melting * fraction)
        keep[1, r] = skin
        keep[2, r] = fraction
        state[0, r] = cover - step * melting
        state[2, r] = step * (gain[r] - 0.5 * melting)
        state[3, r] = skin + step * (air[r] - skin)
        return carry

    def pool(r, carry=0):
        drained = keep[0, r]
        pond = field(4, r) + 0.5 * drained
        state[4, r] = pond
        outflow[0, r] = 0.35 * wet(r) * pond
        thick = field(1, r)
        state[1, r] = thick - drained
        keep[0, r] = softplus(thick) + 0.2
        return carry

    def finish(r, carry=0):
        ocean, snow, skin, fraction = field(5, r), field(2, r), keep[1, r], keep[2, r]
        step = 0.5 * wet(r)
        warm = air[r]
        flux = step * ((ocean - skin) / (keep[0, r] + 0.5 * softplus(snow)))
        cover = state[0, r] + flux
        thick = state[1, r] + 0.5 * flux
        snow = state[2, r] + snow
        skin = state[3, r] + 0.1 * flux
        ocean = ocean + step * (0.2 * (warm - ocean)) - 0.1 * flux * fraction
        conduction = (ocean - skin) / (softplus(thick) + 0.5 * softplus(snow) + 0.2)
        melting = softplus(skin)
        fraction = sigmoid(cover)
        drained = melting * fraction
        state[0, r] = cover + step * (conduction - melting)
        state[1, r] = thick + step * (0.5 * conduction - drained)
        state[2, r] = snow + step * (gain[r] - 0.5 * melting)
        state[3, r] = skin + step * (warm - skin + 0.1 * conduction)
        state[5, r] = ocean + step * (0.2 * (warm - ocean) - 0.1 * conduction * fraction)
        keep[0, r] = step * (0.5 * drained)
        return carry

    def settle(r):
        pond = state[4, r] + keep[0, r]
        state[4, r] = pond
        outflow[1, r] = 0.35 * wet(r) * pond

    def finish_and_settle(r, carry=0):
        finish(r)
        settle(r)
        return carry

    column = lax.broadcasted_iota(jnp.int32, (8, 768), 1)
    row = lax.broadcasted_iota(jnp.int32, (8, 768), 0)
    down = {dc: k for k, (dr, dc) in enumerate(DIRECTIONS) if dr == 1}
    up = {dc: k for k, (dr, dc) in enumerate(DIRECTIONS) if dr == -1}
    level = {dc: k for k, (dr, dc) in enumerate(DIRECTIONS) if dr == 0}

    def drain(s, r):
        def flow(d):
            if isinstance(r, int) and r + d in (-1, 8):
                return jnp.broadcast_to(rim_in[s, 0 if d < 0 else 1], (8, 768))
            return outflow[s, r + d]

        flows = [flow(d) for d in (-1, 0, 1)]
        codes = [code[r + d] for d in range(3)]

        def sent(number, d):
            return jnp.where(codes[d] == number, flows[d], 0.0)

        sums = {}
        for dc in (-1, 0, 1):
            before = pltpu.roll(jnp.where(row == 7, sent(down[dc], 0), sent(down[dc], 1)), 1, 0)
            after = pltpu.roll(jnp.where(row == 0, sent(up[dc], 2), sent(up[dc], 1)), 7, 0)
            sums[dc] = before + after
            if dc:
                sums[dc] = sums[dc] + sent(level[dc], 1)
        right = jnp.where(column == 0, 0.0, pltpu.roll(sums[1], 1, 1))
        left = jnp.where(column == 767, 0.0, pltpu.roll(sums[-1], 767, 1))
        state[4, r] = state[4, r] - flows[1] + wet(r) * (sums[0] + right + left)

    def drain_first(r, carry=0):
        drain(0, r)
        return carry

    def drain_last(r, carry=0):
        drain(1, r)
        return carry

    pass_on(0)
    share(0, 1 - c).wait_recv()
    melt(0)
    melt(7)
    pass_on(1)
    lax.fori_loop(1, 7, melt, 0)
    for k in (0, 1):
        share_outer(k, 1 - c).wait_recv()
        pool(7 * k)
    start_rim(0)
    share(1, 1 - c).wait_recv()
    pass_on_last()
    lax.fori_loop(1, 7, pool, 0)
    wait_edges()
    lax.fori_loop(1, 7, drain_first, 0)
    share(2, 1 - c).wait_recv()
    finish(0)
    finish(7)
    wait_rim(0)
    for r in (0, 7):
        drain(0, r)
        settle(r)
    start_rim(1)
    lax.fori_loop(1, 7, finish_and_settle, 0)
    lax.fori_loop(1, 7, drain_last, 0)
    for i in rounds:
        core_copies[i].wait_send()
        remote(pack, pack, plane_send.at[i], plane_recv.at[i], sibling).wait_send()
        depth_copies[i].wait_send()
        remote(pack, pack, gather_send.at[i], gather_recv.at[i], sibling).wait_send()
        share(i, c).wait_send()
    share_outer(0, c).wait_send()
    share_outer(1, c).wait_send()
    wait_rim(1)
    drain(1, 0)
    drain(1, 7)


def solution(mesh):
    hbm = pl.BlockSpec(memory_space=pltpu.MemorySpace.HBM)
    whole = (6, 8, 8, 768)
    f32, i32 = jnp.float32, jnp.int32
    dma = pltpu.SemaphoreType.DMA

    def shards(members, control, air_temp, flow_codes, ocean_mask):
        rows = (8, 8, 768)
        result = pl.pallas_call(
            kernel,
            out_shape=pltpu.VMEM(whole, f32),
            in_specs=[hbm] * 5,
            out_specs=pl.BlockSpec(memory_space=pltpu.VMEM),
            scratch_shapes=[
                pltpu.VMEM(whole, f32), pltpu.VMEM(whole, f32), pltpu.VMEM(whole, f32),
                pltpu.VMEM((3, *rows), f32), pltpu.VMEM((3, PEERS, 8, 384), f32),
                pltpu.VMEM((3, 8, 384), f32), pltpu.VMEM((3, 8, 384), f32),
                pltpu.VMEM((6, 12, 64), f32), pltpu.VMEM(rows, f32), pltpu.VMEM((10, 8, 768), i32),
                pltpu.VMEM(rows, i32), pltpu.VMEM(rows, f32), pltpu.VMEM((3, *rows), f32),
                pltpu.VMEM((SUBSTEPS, 8, 8, 768), f32),
                pltpu.VMEM((SUBSTEPS, 2, 1, 768), f32), pltpu.VMEM((SUBSTEPS, 2, 1, 768), f32),
                dma((6,)), *[dma((3,))] * 10, dma((3, 2)), dma((3, 2)),
                dma((PEERS,)),
                dma((2,)), dma((2,)),
            ],
            compiler_params=pltpu.CompilerParams(
                collective_id=0, has_side_effects=True, vmem_limit_bytes=VMEM_LIMIT),
            name="recentre_advance",
        )(
            members.reshape(whole), jnp.swapaxes(control, 1, 2), air_temp.reshape(rows),
            flow_codes.reshape(rows), ocean_mask.reshape(rows),
        )
        return result.reshape(1, 6, 64, 768)

    tiles = P("tile", None)
    return jax.shard_map(
        shards, mesh=mesh,
        in_specs=(P("mem", None, "tile", None), P(None, "tile", "mem"), tiles, tiles, tiles),
        out_specs=P("mem", None, "tile", None), check_vma=False)
```

```python
import jax
import jax.numpy as jnp
from jax import lax
from jax.experimental import pallas as pl
from jax.experimental.pallas import tpu as pltpu
from jax.sharding import PartitionSpec as P

MESH = pl.DeviceIdType.MESH
SUBSTEPS = 2
VMEM_LIMIT = 56 * 1024 * 1024
MEMBERS = 64
DIRECTIONS = ((0, 1), (1, 1), (1, 0), (1, -1), (0, -1), (-1, -1), (-1, 0), (-1, 1))
STEPS = sorted(
    ((dx, dy) for dx in range(4) for dy in range(4)),
    key=lambda s: -(min(s[0], 4 - s[0]) + min(s[1], 4 - s[1])),
)
PEERS = len(STEPS) - 1


def softplus(v):
    return jnp.maximum(v, 0.0) + jnp.log1p(jnp.exp(-jnp.abs(v)))


def sigmoid(v):
    return 1.0 / (1.0 + jnp.exp(-v))


def block(field, part):
    columns = pl.ds(pl.multiple_of((part % 2) * 384, 128), 384)
    return field.at[part // 2, :, columns]


def of_core(i, c):
    return (3 * c, 4 - 3 * c, 5 - 3 * c)[i]


def kernel(
    members, control, air_temp, flow_codes, ocean_mask, state,
    own, raw, shift, core_in, plane_in, depth_out, depth_in, strip, air, code, mask, gain, keep, outflow, rim, rim_in,
    local_sem, core_send, core_recv, plane_send, plane_recv, depth_send, depth_recv,
    gather_send, gather_recv, share_send, share_recv, edge_send, edge_recv, plane_ready, depth_near, depth_ready, last_recv, outer_send, outer_recv,
):
    m, t = lax.axis_index("mem"), lax.axis_index("tile")
    x, y, z, c = m // 16, (m // 4) % 4, (m // 2) % 2, m % 2

    def device(x, y, z, c):
        return (((x * 4 + y) * 2 + z) * 2 + c, t)

    sibling = device(x, y, z, 1 - c)
    far = device(x, y, 1 - z, c)
    here = x * 4 + y
    to = [((x + dx) % 4, (y + dy) % 4) for dx, dy in STEPS]
    come = [((x + 4 - dx) % 4, (y + 4 - dy) % 4) for dx, dy in STEPS]
    goal = [a * 4 + b for a, b in to]
    origin = [a * 4 + b for a, b in come]
    above, below = (m, jnp.maximum(t - 1, 0)), (m, jnp.minimum(t + 1, 7))
    has_above, has_below = t > 0, t < 7

    zz = z * 8 + t

    def along(step):
        place = (zz + step) % 16
        return (((x * 4 + y) * 2 + place // 8) * 2 + c, place % 8)

    def greet(sem, target):
        pl.semaphore_signal(sem, inc=1, device_id=target, device_id_type=MESH)

    row_peers = [device((x + d) % 4, y, z, c) for d in (2, 1, 3)]
    column_peers = [device(x, (y + d) % 4, z, c) for d in (2, 1, 3)]
    near = (along(2), along(14))
    barrier = pltpu.get_barrier_semaphore()
    for target in (*near, *row_peers, *column_peers, sibling):
        greet(barrier, target)

    @pl.when(has_above)
    def _():
        greet(barrier, above)

    @pl.when(has_below)
    def _():
        greet(barrier, below)

    loads = [
        pltpu.make_async_copy(s, d, local_sem.at[i])
        for i, (s, d) in enumerate((
            (members, own), (control, strip), (air_temp, air), (ocean_mask, mask),
            (flow_codes, code.at[pl.ds(1, 8)]), (members, raw),
        ))
    ]
    for copy in loads[:2]:
        copy.start()

    loads[0].wait()
    loads[1].wait()
    tile_at = jnp.minimum((12 * m) // 128, 4)
    span = pl.ds(pl.multiple_of(tile_at * 128, 128), 256)
    lane = lax.broadcasted_iota(jnp.int32, (12, 256), 1) + 128 * tile_at - 12 * m
    spread = jnp.where(lane == lax.broadcasted_iota(jnp.int32, (12, 256), 0), -float(MEMBERS), 0.0)
    for f in range(6):
        placed = lax.dot_general(
            strip[f], spread, (((0,), (0,)), ((), ())),
            precision=lax.Precision.HIGHEST, preferred_element_type=jnp.float32)
        for r in range(8):
            own[f, r, :, span] = own[f, r, :, span] + placed[8 * r:8 * r + 8]
    for copy in loads[2:]:
        copy.start()
    extra = jnp.where(has_above, 1, 0) + jnp.where(has_below, 1, 0)
    pl.semaphore_wait(barrier, 9 + extra)
    for target in row_peers:
        greet(plane_ready, target)
    for target in near:
        greet(depth_near, target)

    def remote(src, dst, send, recv, target):
        return pltpu.make_async_remote_copy(
            src_ref=src, dst_ref=dst, send_sem=send, recv_sem=recv, device_id=target, device_id_type=MESH)

    def pair(source, goal_, slot):
        return (
            remote(source[0], goal_[1], edge_send.at[slot, 0], edge_recv.at[slot, 0], above),
            remote(source[1], goal_[0], edge_send.at[slot, 1], edge_recv.at[slot, 1], below),
        )

    def start_pair(upward, downward):
        pl.when(has_above)(upward.start)
        pl.when(has_below)(downward.start)

    def wait_pair(upward, downward):
        @pl.when(has_above)
        def _():
            upward.wait_send()
            downward.wait_recv()

        @pl.when(has_below)
        def _():
            downward.wait_send()
            upward.wait_recv()

    code_pair = pair((code.at[1], code.at[8]), (code.at[0], code.at[9]), 0)
    rim_pairs = [
        pair((rim.at[s, 0], rim.at[s, 1]), (rim_in.at[s, 0], rim_in.at[s, 1]), 1 + s) for s in range(SUBSTEPS)
    ]

    def start_rim(s):
        rim[s, 0] = outflow[s, 0, 0:1]
        rim[s, 1] = outflow[s, 7, 7:8]
        start_pair(*rim_pairs[s])

    def wait_rim(s):
        wait_pair(*rim_pairs[s])

    def wait_edges():
        wait_pair(*code_pair)

    rounds = range(3)
    pack = plane_in.at[0]

    core_copies = [
        remote(own.at[of_core(i, 1 - c)], core_in.at[i], core_send.at[i], core_recv.at[i], sibling)
        for i in rounds
    ]
    for copy in core_copies:
        copy.start()

    order = [sorted(range(PEERS + 1), key=lambda j: (0 not in STEPS[j] or j == PEERS, j))] + [range(PEERS + 1)] * 2
    for i in rounds:
        core_copies[i].wait_recv()
        for j in order[i]:
            if i == 0 and j == order[0][6]:
                pl.semaphore_wait(plane_ready, 3)
            mine = block(core_in.at[i], goal[j])
            mine[...] = mine[...] + block(own.at[of_core(i, c)], goal[j])[...]
            if j < PEERS:
                remote(mine, plane_in.at[i, j], plane_send.at[i], plane_recv.at[i], device(*to[j], z, c)).start()

        if i == 0:
            pl.semaphore_wait(depth_near, 2)
            greet(depth_ready, along(12))

    for i in (2, 3, 4, 5):
        loads[i].wait()
    for r in range(8):
        gain[r] = 0.3 * sigmoid(-air[r])

    for side, edge, missing in ((0, 0, t == 0), (1, 9, t == 7)):
        @pl.when(missing)
        def _():
            code[edge] = jnp.full((8, 768), -1, jnp.int32)
            for s in range(SUBSTEPS):
                rim_in[s, side] = jnp.zeros((1, 768), jnp.float32)

    start_pair(*code_pair)

    depth_copies = [
        remote(depth_out.at[i], depth_in.at[i], depth_send.at[i], depth_recv.at[i], far) for i in rounds
    ]
    for i in rounds:
        remote(pack, pack, plane_send.at[i], plane_recv.at[i], sibling).wait_recv()
        total = block(core_in.at[i], here)[...]
        for j in range(PEERS):
            total = total + plane_in[i, j]
        depth_out[i] = total
        if i == 0:
            pl.semaphore_wait(depth_ready, 1)
        depth_copies[i].start()

    for i in rounds:
        depth_copies[i].wait_recv()
        mine = block(shift.at[of_core(i, c)], here)
        mine[...] = (depth_out[i] + depth_in[i]) * (-1.0 / MEMBERS)
        for j in range(PEERS):
            landed = gather_recv.at[i] if i < 2 else last_recv.at[j]
            remote(mine, mine, gather_send.at[i], landed, device(*to[j], z, c)).start()
        if i == 2:
            remote(mine, mine, share_send.at[i], share_recv.at[i], sibling).start()

    def share(i, c):
        part = shift.at[of_core(i, c)]
        if i == 1:
            part = shift.at[of_core(i, c), pl.ds(1, 6)]
        return remote(part, part, share_send.at[i], share_recv.at[i], sibling)

    def share_outer(k, c):
        part = shift.at[of_core(1, c), 7 * k]
        return remote(part, part, outer_send.at[k], outer_recv.at[k], sibling)

    def pass_on(i):
        remote(pack, pack, gather_send.at[i], gather_recv.at[i], sibling).wait_recv()
        if i == 1:
            share_outer(0, c).start()
            share_outer(1, c).start()
        share(i, c).start()

    def pass_on_last():
        for j in range(PEERS):
            part = block(shift.at[of_core(2, c)], origin[j])
            remote(part, part, share_send.at[2], last_recv.at[j], sibling).wait_recv()
            remote(part, part, share_send.at[2], share_recv.at[2], sibling).start()

    def field(f, r):
        return raw[f, r] + shift[f, r]

    def wet(r):
        return mask[r].astype(jnp.float32)

    def melt(r, carry=0):
        cover, skin = field(0, r), field(3, r)
        step = 0.5 * wet(r)
        melting = softplus(skin)
        fraction = sigmoid(cover)
        keep[0, r] = step * (melting * fraction)
        keep[1, r] = skin
        keep[2, r] = fraction
        state[0, r] = cover - step * melting
        state[2, r] = step * (gain[r] - 0.5 * melting)
        state[3, r] = skin + step * (air[r] - skin)
        return carry

    def pool(r, carry=0):
        drained = keep[0, r]
        pond = field(4, r) + 0.5 * drained
        state[4, r] = pond
        outflow[0, r] = 0.35 * wet(r) * pond
        thick = field(1, r)
        state[1, r] = thick - drained
        keep[0, r] = softplus(thick) + 0.2
        return carry

    def finish(r, carry=0):
        ocean, snow, skin, fraction = field(5, r), field(2, r), keep[1, r], keep[2, r]
        step = 0.5 * wet(r)
        warm = air[r]
        flux = step * ((ocean - skin) / (keep[0, r] + 0.5 * softplus(snow)))
        cover = state[0, r] + flux
        thick = state[1, r] + 0.5 * flux
        snow = state[2, r] + snow
        skin = state[3, r] + 0.1 * flux
        ocean = ocean + step * (0.2 * (warm - ocean)) - 0.1 * flux * fraction
        conduction = (ocean - skin) / (softplus(thick) + 0.5 * softplus(snow) + 0.2)
        melting = softplus(skin)
        fraction = sigmoid(cover)
        drained = melting * fraction
        state[0, r] = cover + step * (conduction - melting)
        state[1, r] = thick + step * (0.5 * conduction - drained)
        state[2, r] = snow + step * (gain[r] - 0.5 * melting)
        state[3, r] = skin + step * (warm - skin + 0.1 * conduction)
        state[5, r] = ocean + step * (0.2 * (warm - ocean) - 0.1 * conduction * fraction)
        keep[0, r] = step * (0.5 * drained)
        return carry

    def settle(r):
        pond = state[4, r] + keep[0, r]
        state[4, r] = pond
        outflow[1, r] = 0.35 * wet(r) * pond

    def finish_and_settle(r, carry=0):
        finish(r)
        settle(r)
        return carry

    column = lax.broadcasted_iota(jnp.int32, (8, 768), 1)
    row = lax.broadcasted_iota(jnp.int32, (8, 768), 0)
    down = {dc: k for k, (dr, dc) in enumerate(DIRECTIONS) if dr == 1}
    up = {dc: k for k, (dr, dc) in enumerate(DIRECTIONS) if dr == -1}
    level = {dc: k for k, (dr, dc) in enumerate(DIRECTIONS) if dr == 0}

    def drain(s, r):
        def flow(d):
            if isinstance(r, int) and r + d in (-1, 8):
                return jnp.broadcast_to(rim_in[s, 0 if d < 0 else 1], (8, 768))
            return outflow[s, r + d]

        flows = [flow(d) for d in (-1, 0, 1)]
        codes = [code[r + d] for d in range(3)]

        def sent(number, d):
            return jnp.where(codes[d] == number, flows[d], 0.0)

        sums = {}
        for dc in (-1, 0, 1):
            before = pltpu.roll(jnp.where(row == 7, sent(down[dc], 0), sent(down[dc], 1)), 1, 0)
            after = pltpu.roll(jnp.where(row == 0, sent(up[dc], 2), sent(up[dc], 1)), 7, 0)
            sums[dc] = before + after
            if dc:
                sums[dc] = sums[dc] + sent(level[dc], 1)
        right = jnp.where(column == 0, 0.0, pltpu.roll(sums[1], 1, 1))
        left = jnp.where(column == 767, 0.0, pltpu.roll(sums[-1], 767, 1))
        state[4, r] = state[4, r] - flows[1] + wet(r) * (sums[0] + right + left)

    def drain_first(r, carry=0):
        drain(0, r)
        return carry

    def drain_last(r, carry=0):
        drain(1, r)
        return carry

    pass_on(0)
    share(0, 1 - c).wait_recv()
    melt(0)
    melt(7)
    pass_on(1)
    lax.fori_loop(1, 7, melt, 0)
    for k in (0, 1):
        share_outer(k, 1 - c).wait_recv()
        pool(7 * k)
    start_rim(0)
    share(1, 1 - c).wait_recv()
    pass_on_last()
    lax.fori_loop(1, 7, pool, 0)
    wait_edges()
    lax.fori_loop(1, 7, drain_first, 0)
    share(2, 1 - c).wait_recv()
    finish(0)
    finish(7)
    wait_rim(0)
    for r in (0, 7):
        drain(0, r)
        settle(r)
    start_rim(1)
    lax.fori_loop(1, 7, finish_and_settle, 0)
    lax.fori_loop(1, 7, drain_last, 0)
    wait_rim(1)
    drain(1, 0)
    drain(1, 7)

    for i in rounds:
        core_copies[i].wait_send()
        remote(pack, pack, plane_send.at[i], plane_recv.at[i], sibling).wait_send()
        depth_copies[i].wait_send()
        remote(pack, pack, gather_send.at[i], gather_recv.at[i], sibling).wait_send()
        share(i, c).wait_send()
    share_outer(0, c).wait_send()
    share_outer(1, c).wait_send()


def solution(mesh):
    hbm = pl.BlockSpec(memory_space=pltpu.MemorySpace.HBM)
    whole = (6, 8, 8, 768)
    f32, i32 = jnp.float32, jnp.int32
    dma = pltpu.SemaphoreType.DMA

    def shards(members, control, air_temp, flow_codes, ocean_mask):
        rows = (8, 8, 768)
        result = pl.pallas_call(
            kernel,
            out_shape=pltpu.VMEM(whole, f32),
            in_specs=[hbm] * 5,
            out_specs=pl.BlockSpec(memory_space=pltpu.VMEM),
            scratch_shapes=[
                pltpu.VMEM(whole, f32), pltpu.VMEM(whole, f32), pltpu.VMEM(whole, f32),
                pltpu.VMEM((3, *rows), f32), pltpu.VMEM((3, PEERS, 8, 384), f32),
                pltpu.VMEM((3, 8, 384), f32), pltpu.VMEM((3, 8, 384), f32),
                pltpu.VMEM((6, 12, 64), f32), pltpu.VMEM(rows, f32), pltpu.VMEM((10, 8, 768), i32),
                pltpu.VMEM(rows, i32), pltpu.VMEM(rows, f32), pltpu.VMEM((3, *rows), f32),
                pltpu.VMEM((SUBSTEPS, 8, 8, 768), f32),
                pltpu.VMEM((SUBSTEPS, 2, 1, 768), f32), pltpu.VMEM((SUBSTEPS, 2, 1, 768), f32),
                dma((6,)), *[dma((3,))] * 10, dma((3, 2)), dma((3, 2)),
                *[pltpu.SemaphoreType.REGULAR] * 3, dma((PEERS,)),
                dma((2,)), dma((2,)),
            ],
            compiler_params=pltpu.CompilerParams(
                collective_id=0, has_side_effects=True, vmem_limit_bytes=VMEM_LIMIT),
            name="recentre_advance",
        )(
            members.reshape(whole), jnp.swapaxes(control, 1, 2), air_temp.reshape(rows),
            flow_codes.reshape(rows), ocean_mask.reshape(rows),
        )
        return result.reshape(1, 6, 64, 768)

    tiles = P("tile", None)
    return jax.shard_map(
        shards, mesh=mesh,
        in_specs=(P("mem", None, "tile", None), P(None, "tile", "mem"), tiles, tiles, tiles),
        out_specs=P("mem", None, "tile", None), check_vma=False)
```
